32 devices in a mesh: dp: 4 (over y, x), tensor: 8 (over z, core).
Axes of the slice: x: 2, y: 2, z: 4, core: 2. Of those that a mesh axis runs over, the one named last changes fastest.
Arguments:
- page_pool: bfloat16 [768, 1024, 256], P('dp', 'tensor'), may hold values from -5 to 5
- page_table: int32 [16, 64], P('dp'), may hold values from 0 to 191, as said below
- destination: int32 [16], replicated, may hold values from 0 to 15, as said below
- cache_len: int32 [16], replicated, may hold values from 2048 to 4096, as said below
- new_tokens: bfloat16 [16, 8192, 384], P('dp', 'tensor'), may hold values from -32 to 32
- residual_in: bfloat16 [8192, 2048], P(('dp', 'tensor')), may hold values from -48 to 48
- out_weight: bfloat16 [2048, 2048], P('tensor'), may hold values from -0.5 to 0.5
- norm_gain: float32 [2048], replicated, may hold values from 0.5 to 1.5
- routes: int32 [8192, 6], P(('dp', 'tensor')), may hold values from 0 to 63, all different within a row; in each aligned block of 256 rows (0 to 255, 256 to 511, ...) at most 32 rows name the same one
- route_gates: float32 [8192, 6], P(('dp', 'tensor')), may hold values from 0.1 to 1
- expert_gate: bfloat16 [64, 2048, 1408], P('tensor', None, 'dp'), may hold values from -0.125 to 0.125
- expert_up: bfloat16 [64, 2048, 1408], P('tensor', None, 'dp'), may hold values from -0.125 to 0.125
- expert_down: bfloat16 [64, 1408, 2048], P('tensor', 'dp'), may hold values from -0.15625 to 0.15625
Outputs:
- layer_out: float32 [8192, 2048], P(('dp', 'tensor'))
The draws below stay inside these ranges and needn't reach their ends.
Inputs may be any that keep to these rules, and one draw needn't show every extreme that they name: `page_table`: each request names pages of its own dp index's pool of 192 pages; requests 2m and 2m + 1 of a dp index share the first half of their 64 pages, and no other page is named twice within a dp index. `destination`: A permutation of the serving slots; each dp index sends exactly one of its 4 requests to a slot of each other dp index and keeps the others in their own slots. `cache_len`: some request has exactly 4096 cached positions. `routes`: in the rows of one device (256 tokens) no expert is named more than 32 times.
All inputs are finite; a program needn't handle non-finite values.
Results may differ from the reference program's by a relative error of at most 0.004.
Values may be sent and summed in bfloat16 or wider, within the bound.
A program may use at most 256 MiB of HBM per device.

```python
import math
import jax
import jax.numpy as jnp
import numpy as np
from jax import lax

D = 2048
HEADS = 16
HD = 128
EXPERTS = 64
FFE = 1408
TOP = 6
SPAN = 512
REQ_DEV = 4
PAGE = 64
PAGES_REQ = 64
REQUESTS = 16
TOKENS = 8192
TOK_DEV = 256
CACHE = 4096
POOL = 192
CAP = 32
FFE_DEV = 352
N_DP = 4


def draw_page_table(key, part):
    half_pages = PAGES_REQ // 2
    group_keys = jax.random.split(key, N_DP)

    def one_group(group_key):
        return jax.random.permutation(group_key, POOL)
    shuffled = jax.vmap(one_group)(group_keys).reshape(N_DP, REQ_DEV // 2, 3, half_pages)
    prefix = shuffled[:, :, 0]
    first_table = jnp.concatenate([prefix, shuffled[:, :, 1]], axis=2)
    second_table = jnp.concatenate([prefix, shuffled[:, :, 2]], axis=2)
    table = jnp.stack([first_table, second_table], axis=2)
    return table.reshape(REQUESTS, PAGES_REQ).astype(jnp.int32)


def draw_destination(key, part):
    group_keys = jax.random.split(key, N_DP)

    def one_group(group_key):
        return jax.random.permutation(group_key, REQ_DEV)
    order = jax.vmap(one_group)(group_keys).astype(jnp.int32)
    group_ids = jnp.arange(N_DP, dtype=jnp.int32)
    steps_ids = jnp.arange(N_DP - 1, dtype=jnp.int32)
    staying = group_ids[:, None] * REQ_DEV + jnp.arange(REQ_DEV, dtype=jnp.int32)[None, :]
    target = (group_ids[:, None] + 1 + steps_ids[None, :]) % N_DP
    target_slot = order[target, steps_ids[None, :]]
    movers = order[:, :N_DP - 1]
    moved = staying.at[group_ids[:, None], movers].set(target * REQ_DEV + target_slot)
    return moved.reshape(REQUESTS).astype(jnp.int32)


def draw_cache_len(key, part):
    key_lengths, key_pick = jax.random.split(key)
    lengths = jax.random.randint(key_lengths, (REQUESTS,), CACHE // 2, CACHE + 1).astype(jnp.int32)
    longest = jax.random.randint(key_pick, (), 0, REQUESTS)
    return lengths.at[longest].set(CACHE).astype(jnp.int32)


def draw_new_tokens(key, part):
    key_query, key_keys, key_values = jax.random.split(key, 3)
    shape = (REQUESTS, HEADS, SPAN, HD)
    queries = jnp.clip(2.0 * jax.random.normal(key_query, shape, jnp.float32), -8.0, 8.0)
    keys_drawn = jnp.clip(jax.random.normal(key_keys, shape, jnp.float32), -5.0, 5.0)
    values = jnp.clip(jax.random.normal(key_values, shape, jnp.float32), -5.0, 5.0)
    stacked = jnp.concatenate([queries, keys_drawn, values], axis=3)
    return stacked.reshape(REQUESTS, HEADS * SPAN, 3 * HD).astype(jnp.bfloat16)


def draw_residual_in(key, part):
    key_rows, key_cols, key_values = jax.random.split(key, 3)
    col_scale = jnp.exp(jax.random.uniform(key_cols, (1, D), jnp.float32, math.log(0.3), math.log(3.0)))
    row_scale = jnp.exp(jax.random.uniform(key_rows, (TOKENS, 1), jnp.float32, math.log(0.4), math.log(4.0)))
    values = jnp.clip(jax.random.normal(key_values, (TOKENS, D), jnp.float32), -4.0, 4.0)
    return (values * col_scale * row_scale).astype(jnp.bfloat16)


def steps_of(key, extent, shards, low, high):
    loudness, own = 1.0, jax.random.fold_in(key, 6)
    for dim, shards_of in shards:
        draws = jnp.exp(jax.random.uniform(jax.random.fold_in(own, dim), (shards_of,), jnp.float32, low / len(shards), high / len(shards)))
        loudness = loudness * jnp.repeat(draws, extent[dim] // shards_of).reshape([-1 if axis == dim else 1 for axis in range(len(extent))])
    return loudness


def assign_block(stream_key, own, number, rows, amount, top, bound, slope):
    sequence = jax.random.permutation(stream_key, amount)
    packed, common = shares(amount, rows * top, bound, slope, True), shares(amount, rows * top, bound, slope, False)
    places = jnp.arange(amount)

    def named(tallies, turn):
        used = int((tallies > 0).sum())
        fixed = max(1, used // 4)
        passed = fixed + (places - fixed + turn * (used - fixed)) % max(1, amount - fixed)
        return jnp.zeros((amount,), jnp.int32).at[sequence[jnp.where(places < fixed, places, passed)]].set(jnp.asarray(tallies, jnp.int32))

    tallies = jnp.where(number % 4 == 0, named(packed, number // 4), named(common, number - number // 4 - 1))
    mixed = jax.random.permutation(jax.random.fold_in(own, 3), amount)
    donor, receiver = mixed[0:amount // 2 * 2:2], mixed[1:amount // 2 * 2:2]
    room = jnp.minimum(tallies[donor] - 1, bound - tallies[receiver]) // 2
    room = jnp.where((donor == sequence[0]) | (receiver == sequence[0]) | (tallies[receiver] == 0), 0, jnp.maximum(room, 0))
    passed = jax.random.randint(jax.random.fold_in(own, 4), (amount // 2,), 0, 1 << 20) % (room + 1)
    tallies = tallies.at[donor].add(-passed).at[receiver].add(passed)
    items = jnp.searchsorted(jnp.cumsum(tallies), jnp.arange(rows * top), side="right").astype(jnp.int32)
    table = items.reshape(top, rows).T
    table = table[jax.random.permutation(jax.random.fold_in(own, 1), rows)]
    turn = jax.random.randint(jax.random.fold_in(own, 2), (rows, 1), 0, top)
    return jnp.take_along_axis(table, (jnp.arange(top)[None, :] + turn) % top, axis=1)


def shares(count, total, bound, skew, full):
    weights = [(1 << 20) // math.isqrt(rank ** skew) + 1 for rank in range(1, count + 1)]
    largest = bound if full else min(bound, max(-(-total // count), total * weights[0] // sum(weights)))
    least = 1 if total - largest >= count - 1 else 0
    given, rest = [largest] + [least] * (count - 1), total - largest - least * (count - 1)
    while rest > 0:
        candidates = [i for i in range(1, count) if given[i] < largest] or [i for i in range(1, count) if given[i] < bound]
        pool, remaining = sum([weights[i] for i in candidates]), rest
        for i in candidates:
            addition = min(bound - given[i], max(1, remaining * weights[i] // pool), rest)
            given[i] = given[i] + addition
            rest = rest - addition
    return np.array(given)


def scatter_about(rng, dims, scale, most, cuts=(), held_as=jnp.bfloat16):
    gain = steps_of(rng, dims, cuts, -0.22, 0.18) if cuts else 1.0
    values = jax.random.normal(rng, dims, jnp.float32) * scale * gain
    return jnp.minimum(jnp.maximum(values, -most), most).astype(held_as)


def setup_inputs(seed: int = 0) -> dict:
    keys = jax.random.split(jax.random.key(seed), 14)
    page_pool = scatter_about(keys[0], (N_DP * POOL, HEADS * PAGE, 2 * HD), 1.0, 5.0, ((0, 4), (1, 8)))
    page_table = draw_page_table(jax.random.fold_in(keys[13], 71), 0)
    destination = draw_destination(jax.random.fold_in(keys[13], 71), 0)
    cache_len = draw_cache_len(jax.random.fold_in(keys[13], 71), 0)
    new_tokens = draw_new_tokens(jax.random.fold_in(keys[13], 71), 0)
    residual_in = draw_residual_in(jax.random.fold_in(keys[13], 71), 0)
    out_weight = scatter_about(keys[6], (HEADS * HD, D), HD ** -0.5, 0.5, ((0, 8),))
    norm_gain = jnp.clip(1.0 + 0.1 * jax.random.normal(keys[7], (D,), jnp.float32), 0.5, 1.5)
    routes_keys = jax.random.split(jax.random.fold_in(keys[8], 1), TOKENS // TOK_DEV)
    routes_turns = jax.random.permutation(jax.random.fold_in(keys[8], 3), TOKENS // TOK_DEV)
    routes = jax.vmap(lambda own, number: assign_block(jax.random.fold_in(keys[8], 2), own, number, TOK_DEV, EXPERTS, TOP, CAP, 2))(routes_keys, routes_turns).reshape((TOKENS, TOP))
    route_gates = jnp.clip(jnp.exp(math.log(1.0) - 2.3025851 * jax.random.uniform(keys[9], (TOKENS, TOP), jnp.float32) ** steps_of(keys[9], (TOKENS, TOP), ((0, 32),), -0.2, 0.2)), 0.1, 1.0)
    expert_gate = scatter_about(keys[10], (EXPERTS, D, FFE), D ** -0.5, 0.125, ((0, 8), (2, 4)))
    expert_up = scatter_about(keys[11], (EXPERTS, D, FFE), D ** -0.5, 0.125, ((0, 8), (2, 4)))
    expert_down = scatter_about(keys[12], (EXPERTS, FFE, D), FFE ** -0.5, 0.15625, ((0, 8), (1, 4)))
    return {"page_pool": page_pool, "page_table": page_table, "destination": destination, "cache_len": cache_len, "new_tokens": new_tokens, "residual_in": residual_in, "out_weight": out_weight, "norm_gain": norm_gain, "routes": routes, "route_gates": route_gates, "expert_gate": expert_gate, "expert_up": expert_up, "expert_down": expert_down}


def attend_head(cached, fresh_rows, length):
    queries = fresh_rows[:, :HD]
    new_keys = fresh_rows[:, HD:2 * HD]
    new_values = fresh_rows[:, 2 * HD:]
    scale_factor = 1.0 / HD ** 0.5
    cache_scores = jnp.dot(queries, cached[:, :HD].T, preferred_element_type=jnp.float32) * scale_factor
    span_scores = jnp.dot(queries, new_keys.T, preferred_element_type=jnp.float32) * scale_factor
    cache_live = jnp.arange(CACHE, dtype=jnp.int32)[None, :] < length
    positions = jnp.arange(SPAN, dtype=jnp.int32)
    span_live = positions[None, :] <= positions[:, None]
    cache_scores = jnp.where(cache_live, cache_scores, -1e+30)
    span_scores = jnp.where(span_live, span_scores, -1e+30)
    maximum = jnp.maximum(lax.optimization_barrier(jnp.max(cache_scores, axis=1)), lax.optimization_barrier(jnp.max(span_scores, axis=1)))
    cache_weights = jnp.exp(cache_scores - maximum[:, None])
    span_weights = jnp.exp(span_scores - maximum[:, None])
    denominator = lax.optimization_barrier(jnp.sum(cache_weights, axis=1)) + lax.optimization_barrier(jnp.sum(span_weights, axis=1))
    weighted = jnp.dot(cache_weights.astype(jnp.bfloat16), cached[:, HD:], preferred_element_type=jnp.float32)
    weighted = weighted + jnp.dot(span_weights.astype(jnp.bfloat16), new_values, preferred_element_type=jnp.float32)
    return (weighted / denominator[:, None]).astype(jnp.bfloat16)

def reference(page_pool, page_table, destination, cache_len, new_tokens, residual_in, out_weight, norm_gain, routes, route_gates, expert_gate, expert_up, expert_down):
    slot_ids = jnp.arange(REQUESTS, dtype=jnp.int32)
    inverse = jnp.zeros((REQUESTS,), jnp.int32).at[destination].set(slot_ids)

    def one_slot(slot_index):
        home_request = inverse[slot_index]
        home_group = home_request // REQ_DEV
        gathered = page_pool[home_group * POOL + page_table[home_request]]
        cached = gathered.reshape(PAGES_REQ, HEADS, PAGE, 2 * HD).transpose(1, 0, 2, 3).reshape(HEADS, CACHE, 2 * HD)
        fresh_rows = new_tokens[slot_index].reshape(HEADS, SPAN, 3 * HD)
        length = cache_len[home_request]

        def one_head(operands):
            return attend_head(operands[0], operands[1], length)
        heads_out = lax.map(one_head, (cached, fresh_rows))
        return heads_out.transpose(1, 0, 2).reshape(SPAN, HEADS * HD)
    attended = lax.map(one_slot, slot_ids).reshape(TOKENS, HEADS * HD)
    projected = jnp.dot(attended, out_weight, preferred_element_type=jnp.float32)
    hidden = residual_in.astype(jnp.float32) + projected
    normed = (hidden * lax.rsqrt(lax.optimization_barrier(jnp.mean(hidden * hidden, axis=1, keepdims=True)) + 1e-06) * norm_gain).astype(jnp.bfloat16)
    flat_routes = routes.reshape(-1)
    flat_gates = route_gates.reshape(-1)
    most_rows = CAP * (TOKENS // TOK_DEV)

    def add_expert(running, expert):
        named = flat_routes == expert
        pair_hits = jnp.nonzero(named, size=most_rows, fill_value=0)[0].astype(jnp.int32)
        live_rows = jnp.arange(most_rows, dtype=jnp.int32) < jnp.sum(named.astype(jnp.int32))
        token_ids = pair_hits // TOP
        chosen_rows = normed[token_ids]
        gate_part = jnp.dot(chosen_rows, expert_gate[expert], preferred_element_type=jnp.float32)
        up_part = jnp.dot(chosen_rows, expert_up[expert], preferred_element_type=jnp.float32)
        active = (jax.nn.silu(gate_part) * up_part).astype(jnp.bfloat16)
        blocks = active.reshape(most_rows, N_DP, FFE_DEV).astype(jnp.float32)
        down_blocks = expert_down[expert].reshape(N_DP, FFE_DEV, D).astype(jnp.float32)
        partial_value = jnp.einsum('rbf,bfd->rbd', blocks, down_blocks)
        rounded = lax.optimization_barrier(partial_value.astype(jnp.bfloat16))
        expert_out = lax.optimization_barrier(jnp.sum(rounded.astype(jnp.float32), axis=1))
        gate_weight = jnp.where(live_rows, flat_gates[pair_hits], 0.0)
        running = running.at[token_ids].add(gate_weight[:, None] * expert_out)
        return (running, expert)
    routed = lax.scan(add_expert, jnp.zeros((TOKENS, D), jnp.float32), jnp.arange(EXPERTS, dtype=jnp.int32))[0]
    return (hidden + routed).astype(jnp.float32)
```

```python
import jax
import jax.numpy as jnp
from jax import lax
from jax.experimental import pallas as pl
from jax.experimental.pallas import tpu as pltpu
from jax.sharding import PartitionSpec as P

HEADS = 16
HD = 128
EXPERTS = 64
TOP = 6
PAGE = 64


def swapped(array, axis, stride):
    return lax.ppermute(array, axis, [(i, i ^ 1 << stride) for i in range(lax.axis_size(axis))])


def local_attention(queries, cached, fresh_rows, length, cache_offset, span_offset):
    head_size = queries.shape[1]
    span_len = queries.shape[0]
    page_count = cached.shape[0]
    page_rows = cached.shape[1]
    scale_factor = 1.0 / head_size**0.5
    cache_scores = jnp.einsum(
        "qd,pjd->qpj", queries, cached[:, :, :head_size], preferred_element_type=jnp.float32
    )
    cache_scores = cache_scores.reshape(span_len, page_count * page_rows) * scale_factor
    page_ids = jnp.arange(page_count, dtype=jnp.int32)[:, None]
    row_ids = jnp.arange(page_rows, dtype=jnp.int32)[None, :]
    positions = (page_ids * PAGE + cache_offset + row_ids).reshape(-1)
    cache_scores = jnp.where(positions[None, :] < length, cache_scores, -1e30)
    new_keys = fresh_rows[:, head_size : 2 * head_size]
    new_values = fresh_rows[:, 2 * head_size :]
    span_scores = jnp.dot(queries, new_keys.T, preferred_element_type=jnp.float32) * scale_factor
    key_pos = span_offset + jnp.arange(fresh_rows.shape[0], dtype=jnp.int32)
    query_pos = jnp.arange(span_len, dtype=jnp.int32)
    span_scores = jnp.where(key_pos[None, :] <= query_pos[:, None], span_scores, -1e30)
    maximum = jnp.maximum(jnp.max(cache_scores, axis=1), jnp.max(span_scores, axis=1))
    cache_weights = jnp.exp(cache_scores - maximum[:, None])
    span_weights = jnp.exp(span_scores - maximum[:, None])
    denominator = jnp.sum(cache_weights, axis=1) + jnp.sum(span_weights, axis=1)
    rounded = cache_weights.astype(jnp.bfloat16).reshape(span_len, page_count, page_rows)
    weighted = jnp.einsum(
        "qpj,pjd->qd", rounded, cached[:, :, head_size:], preferred_element_type=jnp.float32
    )
    weighted = weighted + jnp.dot(
        span_weights.astype(jnp.bfloat16), new_values, preferred_element_type=jnp.float32
    )
    return (weighted, maximum, denominator)


def run_experts(slot_rows, expert_gate, expert_up, expert_down):
    gate_part = jnp.einsum(
        "secd,edf->secf", slot_rows, expert_gate, preferred_element_type=jnp.float32
    )
    up_part = jnp.einsum("secd,edf->secf", slot_rows, expert_up, preferred_element_type=jnp.float32)
    active = (jax.nn.silu(gate_part) * up_part).astype(jnp.bfloat16)
    return jnp.einsum("secf,efd->secd", active, expert_down, preferred_element_type=jnp.float32)


def shards(
    page_pool,
    page_table,
    destination,
    cache_len,
    new_tokens,
    residual_in,
    out_weight,
    norm_gain,
    routes,
    route_gates,
    expert_gate,
    expert_up,
    expert_down,
):
    tensor_size = lax.axis_size("tensor")
    group_count = lax.axis_size("dp")
    split_ways = max(1, tensor_size // HEADS)
    heads_here = max(1, HEADS // tensor_size)
    side_index = lax.axis_index("tensor") % split_ways
    group_index = lax.axis_index("dp")
    requests_here = page_table.shape[0]
    first_home = group_index * requests_here
    home_dest = lax.dynamic_slice_in_dim(destination, first_home, requests_here)
    dest_group = home_dest // requests_here
    group_ids = jnp.arange(group_count, dtype=jnp.int32)
    request_ids = jnp.arange(requests_here, dtype=jnp.int32)
    leaving = dest_group[None, :] == group_ids[:, None]
    chosen = jnp.sum(jnp.where(leaving, request_ids[None, :], 0), axis=1)
    chosen = jnp.where(group_ids == group_index, 0, chosen)
    outgoing = page_pool[page_table[chosen]]
    arrived = lax.all_to_all(outgoing, "dp", split_axis=0, concat_axis=0, tiled=True)
    inverse = (
        jnp.zeros_like(destination)
        .at[destination]
        .set(jnp.arange(destination.shape[0], dtype=jnp.int32))
    )
    served = lax.dynamic_slice_in_dim(inverse, first_home, requests_here)
    source = served // requests_here
    resident = source == group_index
    local_pages = page_pool[page_table[jnp.where(resident, served - first_home, 0)]]
    dense_cache = jnp.where(resident[:, None, None, None], local_pages, arrived[source])
    lengths = cache_len[served]
    fresh_per = new_tokens.shape[1] // heads_here
    span_len = fresh_per * split_ways
    rows_per_head = dense_cache.shape[2] // heads_here
    if split_ways == 2:
        own_queries = new_tokens[:, :, :HD]
        other_queries = swapped(own_queries, "tensor", 0)
        lower_half = jnp.where(side_index == 0, own_queries, other_queries)
        upper_half = jnp.where(side_index == 0, other_queries, own_queries)
        queries = jnp.concatenate([lower_half, upper_half], axis=1)[:, None]
    else:
        queries = new_tokens[:, :, :HD].reshape(requests_here, heads_here, span_len, HD)
    head_results = []
    for head_index in range(heads_here):
        head_cache = dense_cache[
            :, :, head_index * rows_per_head : (head_index + 1) * rows_per_head
        ]
        head_fresh = new_tokens[:, head_index * fresh_per : (head_index + 1) * fresh_per]

        def one_request(operands):
            return local_attention(
                operands[0],
                operands[1],
                operands[2],
                operands[3],
                side_index * rows_per_head,
                side_index * fresh_per,
            )

        head_results.append(
            lax.map(one_request, (queries[:, head_index], head_cache, head_fresh, lengths))
        )
    if split_ways == 2:
        weighted, maximum, denominator = head_results[0]
        half_dim = HD // 2
        given_part = lax.dynamic_slice_in_dim(weighted, (1 - side_index) * half_dim, half_dim, 2)
        kept_part = lax.dynamic_slice_in_dim(weighted, side_index * half_dim, half_dim, 2)
        received_part, other_max, other_den = swapped(
            (given_part, maximum, denominator), "tensor", 0
        )
        joint_max = jnp.maximum(maximum, other_max)
        own_scale = jnp.exp(maximum - joint_max)
        theirs = jnp.exp(other_max - joint_max)
        combined = kept_part * own_scale[..., None] + received_part * theirs[..., None]
        attended = combined / (denominator * own_scale + other_den * theirs)[..., None]
        head_out = attended.astype(jnp.bfloat16).reshape(requests_here * span_len, half_dim)
    else:
        outputs = []
        for result in head_results:
            outputs.append((result[0] / result[2][..., None]).astype(jnp.bfloat16))
        head_out = jnp.stack(outputs, axis=2).reshape(requests_here * span_len, heads_here * HD)
    tok_rows = residual_in.shape[0]
    projected = lax.psum_scatter(
        jnp.dot(head_out, out_weight, preferred_element_type=jnp.float32),
        "tensor",
        scatter_dimension=0,
        tiled=True,
    )
    hidden = residual_in.astype(jnp.float32) + projected
    normed = (
        hidden * lax.rsqrt(jnp.mean(hidden * hidden, axis=1, keepdims=True) + 1e-06) * norm_gain
    ).astype(jnp.bfloat16)
    capacity = max(2, tok_rows * TOP * 4 // (3 * EXPERTS))
    flat_routes = routes.reshape(-1)
    pair_count = flat_routes.shape[0]
    expert_ids = jnp.arange(EXPERTS, dtype=jnp.int32)
    one_hot = (flat_routes[:, None] == expert_ids[None, :]).astype(jnp.int32)
    earlier = jnp.cumsum(one_hot, axis=0) - one_hot
    rank_in_expert = jnp.sum(earlier * one_hot, axis=1)
    slot_of_pair = flat_routes * capacity + rank_in_expert
    slot_ids = jnp.arange(EXPERTS * capacity, dtype=jnp.int32)
    matches = slot_of_pair[None, :] == slot_ids[:, None]
    source_pair = jnp.sum(
        jnp.where(matches, jnp.arange(pair_count, dtype=jnp.int32)[None, :], 0), axis=1
    )
    filled = jnp.any(matches, axis=1)
    outgoing_rows = jnp.where(
        filled[:, None], normed[source_pair // TOP], jnp.zeros((), jnp.bfloat16)
    )
    experts_here = expert_gate.shape[0]
    width = normed.shape[1]
    outgoing_rows = outgoing_rows.reshape(tensor_size, experts_here, capacity, width)
    fanned = jnp.broadcast_to(outgoing_rows[None], (group_count,) + outgoing_rows.shape)
    fanned = fanned.reshape((group_count * tensor_size,) + outgoing_rows.shape[1:])
    partial_value = run_experts(
        lax.all_to_all(fanned, ("dp", "tensor"), split_axis=0, concat_axis=0, tiled=True),
        expert_gate,
        expert_up,
        expert_down,
    ).astype(jnp.bfloat16)
    returned = lax.all_to_all(
        partial_value, ("dp", "tensor"), split_axis=0, concat_axis=0, tiled=True
    )
    slot_out = jnp.sum(
        returned.reshape(group_count, EXPERTS * capacity, width).astype(jnp.float32), axis=0
    )
    picked = slot_out[slot_of_pair].reshape(tok_rows, TOP, width)
    routed = jnp.sum(picked * route_gates[:, :, None], axis=1)
    return hidden + routed


def exchanged(blocks, axis):
    return lax.all_to_all(blocks, axis, split_axis=0, concat_axis=0, tiled=True)


def attention_kernel(
    table_ref, length_ref, pool_ref, fresh_ref, out_ref, pages, top, total, arrival, *, heads, step
):
    turn = pl.program_id(0)
    page_count = pages.shape[1]
    span_len = fresh_ref.shape[1] // heads
    scale_factor = 1.4426950408889634 / HD**0.5

    def fetch(request, slot):
        def one_page(page, carry):
            pltpu.make_async_copy(
                pool_ref.at[table_ref[request, page]], pages.at[slot, page], arrival.at[slot]
            ).start()
            return carry

        lax.fori_loop(0, page_count, one_page, 0)

    @pl.when(turn == 0)
    def _():
        fetch(0, 0)

    @pl.when(turn + 1 < pl.num_programs(0))
    def _():
        fetch(turn + 1, (turn + 1) % 2)

    slot = turn % 2
    length = length_ref[turn]

    def query_of(head):
        return fresh_ref[0, head * span_len : (head + 1) * span_len, :HD]

    def scores_of(head, keys):
        return (
            lax.dot_general(
                query_of(head), keys, (((1,), (1,)), ((), ())), preferred_element_type=jnp.float32
            )
            * scale_factor
        )

    def weighted_of(weights, values):
        widened = jnp.concatenate([values, jnp.ones_like(values)], axis=1)
        return jnp.dot(
            weights.astype(jnp.bfloat16), widened, preferred_element_type=jnp.float32
        )

    for head in range(heads):
        rows = slice(head * span_len, (head + 1) * span_len)
        scores = scores_of(head, fresh_ref[0, rows, HD : 2 * HD])
        query_pos = lax.broadcasted_iota(jnp.int32, scores.shape, 0)
        key_pos = lax.broadcasted_iota(jnp.int32, scores.shape, 1)
        scores = jnp.where(key_pos <= query_pos, scores, -1e30)
        largest = jnp.max(scores, axis=1, keepdims=True)
        top[head] = jnp.broadcast_to(largest, top.shape[1:])
        total[head] = weighted_of(jnp.exp2(scores - largest), fresh_ref[0, rows, 2 * HD :])

    pltpu.make_async_copy(
        pool_ref.at[pl.ds(0, page_count)], pages.at[slot], arrival.at[slot]
    ).wait()

    def chunk(index, masked):
        for head in range(heads):
            block = pages[slot, pl.ds(index * step, step), head * PAGE : (head + 1) * PAGE, :]
            block = block.reshape(step * PAGE, 2 * HD)
            scores = scores_of(head, block[:, :HD])
            if masked:
                key_pos = index * (step * PAGE) + lax.broadcasted_iota(jnp.int32, scores.shape, 1)
                scores = jnp.where(key_pos < length, scores, -1e30)
            before = top[head][:, :1]
            largest = jnp.maximum(before, jnp.max(scores, axis=1, keepdims=True))
            weighted = weighted_of(jnp.exp2(scores - largest), block[:, HD:])
            total[head] = total[head] * jnp.exp2(before - largest) + weighted
            top[head] = jnp.broadcast_to(largest, top.shape[1:])

    whole = length // (step * PAGE)

    def one_chunk(index, carry):
        chunk(index, False)
        return carry

    lax.fori_loop(0, whole, one_chunk, 0)

    @pl.when(whole * (step * PAGE) < length)
    def _():
        chunk(whole, True)

    for head in range(heads):
        joined = total[head]
        out_ref[0, :, head * HD : (head + 1) * HD] = (joined[:, :HD] / joined[:, HD:]).astype(
            out_ref.dtype
        )


def paged_attention(page_pool, table, lengths, fresh, heads):
    requests, page_count = table.shape
    span_len = fresh.shape[1] // heads
    step = max(size for size in (1, 2, 4, 8, 16) if page_count % size == 0)
    return pl.pallas_call(
        lambda *refs: attention_kernel(*refs, heads=heads, step=step),
        out_shape=jax.ShapeDtypeStruct((requests, span_len, heads * HD), jnp.bfloat16),
        grid_spec=pltpu.PrefetchScalarGridSpec(
            num_scalar_prefetch=2,
            grid=(requests,),
            in_specs=[
                pl.BlockSpec(memory_space=pl.ANY),
                pl.BlockSpec((1,) + fresh.shape[1:], lambda i, *_: (i, 0, 0)),
            ],
            out_specs=pl.BlockSpec((1, span_len, heads * HD), lambda i, *_: (i, 0, 0)),
            scratch_shapes=[
                pltpu.VMEM((2, page_count) + page_pool.shape[1:], jnp.bfloat16),
                pltpu.VMEM((heads, span_len, HD), jnp.float32),
                pltpu.VMEM((heads, span_len, 2 * HD), jnp.float32),
                pltpu.SemaphoreType.DMA((2,)),
            ],
        ),
        compiler_params=pltpu.CompilerParams(vmem_limit_bytes=48 * 2**20),
    )(table, lengths, page_pool, fresh)


def expert_kernel(
    rank_ref, weight_ref, rows_ref, gate_ref, up_ref, down_ref, out_ref, held, *, capacity
):
    expert = pl.program_id(1)
    sources, experts, tokens = rank_ref.shape
    width = rows_ref.shape[1]

    def placement(source):
        ranks = rank_ref[source]
        places = lax.broadcasted_iota(jnp.int32, (experts, capacity, tokens), 1).astype(jnp.float32)
        hits = jnp.where(ranks[:, None, :] == places, 1.0, 0.0)
        return hits.reshape(experts * capacity, tokens).astype(jnp.bfloat16)

    def slots_of(source):
        return pl.ds(pl.multiple_of(source * capacity, capacity), capacity)

    def rows_of(source):
        return pl.ds(pl.multiple_of(source * tokens, tokens), tokens)

    @pl.when(expert == 0)
    def _():
        def gather(source, carry):
            picked = jnp.dot(
                placement(source), rows_ref[rows_of(source), :], preferred_element_type=jnp.float32
            ).astype(jnp.bfloat16)
            held[:, slots_of(source), :] = picked.reshape(experts, capacity, width)
            return carry

        lax.fori_loop(0, sources, gather, 0)

    chosen = held[expert]
    gate_part = jnp.dot(chosen, gate_ref[0], preferred_element_type=jnp.float32)
    up_part = jnp.dot(chosen, up_ref[0], preferred_element_type=jnp.float32)
    active = (gate_part / (1.0 + jnp.exp(-gate_part)) * up_part).astype(jnp.bfloat16)
    ranks = rank_ref[:, pl.ds(expert, 1), :]
    weights = weight_ref[:, pl.ds(expert, 1), :]
    places = lax.broadcasted_iota(jnp.int32, (sources, capacity, tokens), 1).astype(jnp.float32)
    slot_weight = jnp.sum(jnp.where(ranks == places, weights, 0.0), axis=2, keepdims=True)
    partial_value = jnp.dot(active, down_ref[0], preferred_element_type=jnp.float32)
    scaled = partial_value * slot_weight.reshape(sources * capacity, 1)
    held[expert] = scaled.astype(jnp.bfloat16)

    @pl.when(expert == experts - 1)
    def _():
        def combine(source, carry):
            parts = held[:, slots_of(source), :].reshape(experts * capacity, width)
            out_ref[rows_of(source), :] = lax.dot_general(
                placement(source),
                parts,
                (((0,), (0,)), ((), ())),
                preferred_element_type=jnp.float32,
            ).astype(out_ref.dtype)
            return carry

        lax.fori_loop(0, sources, combine, 0)


def routed_experts(ranks, weights, rows, expert_gate, expert_up, expert_down, capacity):
    sources, experts, tokens = ranks.shape
    width = rows.shape[1]
    hidden_units = expert_gate.shape[2]
    together = max(size for size in (1, 2, 4, 8) if sources % size == 0)
    return pl.pallas_call(
        lambda *refs: expert_kernel(*refs, capacity=capacity),
        out_shape=jax.ShapeDtypeStruct(rows.shape, jnp.bfloat16),
        grid=(sources // together, experts),
        in_specs=[
            pl.BlockSpec((together, experts, tokens), lambda i, j: (i, 0, 0)),
            pl.BlockSpec((together, experts, tokens), lambda i, j: (i, 0, 0)),
            pl.BlockSpec((together * tokens, width), lambda i, j: (i, 0)),
            pl.BlockSpec((1, width, hidden_units), lambda i, j: (j, 0, 0)),
            pl.BlockSpec((1, width, hidden_units), lambda i, j: (j, 0, 0)),
            pl.BlockSpec((1, hidden_units, width), lambda i, j: (j, 0, 0)),
        ],
        out_specs=pl.BlockSpec((together * tokens, width), lambda i, j: (i, 0)),
        scratch_shapes=[pltpu.VMEM((experts, together * capacity, width), jnp.bfloat16)],
        compiler_params=pltpu.CompilerParams(vmem_limit_bytes=60 * 2**20),
    )(ranks, weights, rows, expert_gate, expert_up, expert_down)


def home_shards(
    page_pool,
    page_table,
    destination,
    cache_len,
    new_tokens,
    residual_in,
    out_weight,
    norm_gain,
    routes,
    route_gates,
    expert_gate,
    expert_up,
    expert_down,
):
    both = ("dp", "tensor")
    tensor_index = lax.axis_index("tensor")
    group_index = lax.axis_index("dp")
    heads_here = HEADS // lax.axis_size("tensor")
    requests_here = page_table.shape[0]
    first_home = group_index * requests_here
    group_ids = jnp.arange(requests_here, dtype=jnp.int32)

    home_dest = lax.dynamic_slice_in_dim(destination, first_home, requests_here)
    to_group = (home_dest // requests_here)[None, :] == group_ids[:, None]
    request_of = jnp.sum(jnp.where(to_group, group_ids[None, :], 0), axis=1)
    all_ids = jnp.arange(destination.shape[0], dtype=jnp.int32)
    slot_ids = first_home + group_ids
    served = jnp.sum(
        jnp.where(destination[None, :] == slot_ids[:, None], all_ids[None, :], 0), axis=1
    )
    source = served // requests_here
    slot_of = jnp.sum(
        jnp.where(source[None, :] == group_ids[:, None], group_ids[None, :], 0), axis=1
    )

    fresh = exchanged(new_tokens[slot_of], "dp")
    lengths = cache_len[first_home + request_of]
    attended = paged_attention(page_pool, page_table[request_of], lengths, fresh, heads_here)
    span_len, head_width = attended.shape[1:]
    by_slot = exchanged(attended, "dp")[source]
    by_slot = by_slot.reshape(requests_here * span_len, head_width)

    tok_rows, width = residual_in.shape
    whole_weight = lax.all_gather(out_weight, "tensor", axis=0, tiled=True)
    head_out = lax.all_to_all(by_slot, "tensor", split_axis=0, concat_axis=1, tiled=True)
    projected = jnp.dot(head_out, whole_weight, preferred_element_type=jnp.float32)
    hidden = residual_in.astype(jnp.float32) + projected
    normed = (
        hidden * lax.rsqrt(jnp.mean(hidden * hidden, axis=1, keepdims=True) + 1e-06) * norm_gain
    ).astype(jnp.bfloat16)

    capacity = max(2, tok_rows * TOP * 4 // (3 * EXPERTS))
    experts_here = expert_gate.shape[0]
    all_routes = lax.all_gather(routes.T, both, axis=0, tiled=False)
    all_gates = lax.all_gather(route_gates.T, both, axis=0, tiled=False)
    own_experts = tensor_index * experts_here + jnp.arange(experts_here, dtype=jnp.int32)
    named = all_routes[:, None] == own_experts[None, :, None, None]
    weights = jnp.sum(jnp.where(named, all_gates[:, None], 0.0), axis=2)
    hit = jnp.any(named, axis=2)
    token_ids = jnp.arange(tok_rows, dtype=jnp.int32)
    before = (token_ids[:, None] < token_ids[None, :]).astype(jnp.bfloat16)
    ranks = jnp.einsum(
        "set,tu->seu", hit.astype(jnp.bfloat16), before, preferred_element_type=jnp.float32
    )
    ranks = jnp.where(hit, ranks, -1.0)

    rows = lax.all_gather(normed, both, axis=0, tiled=True)
    partial_value = routed_experts(
        ranks, weights, rows, expert_gate, expert_up, expert_down, capacity
    )
    routed = lax.psum_scatter(partial_value, both, scatter_dimension=0, tiled=True)
    return hidden + routed.astype(jnp.float32)


def solution(mesh):
    sizes = dict(mesh.shape)
    own_heads = HEADS % sizes["tensor"] == 0
    return jax.shard_map(
        home_shards if own_heads else shards,
        mesh=mesh,
        in_specs=(
            P("dp", "tensor", None),
            P("dp", None),
            P(),
            P(),
            P("dp", "tensor", None),
            P(("dp", "tensor"), None),
            P("tensor", None),
            P(),
            P(("dp", "tensor"), None),
            P(("dp", "tensor"), None),
            P("tensor", None, "dp"),
            P("tensor", None, "dp"),
            P("tensor", "dp", None),
        ),
        out_specs=P(("dp", "tensor"), None),
        check_vma=False,
    )
```
